32 devices in a mesh: groups: 2 (over y), trade: 4 (over z), scen: 2 (over x), hz: 2 (over core).
Axes of the slice: x: 2, y: 2, z: 4, core: 2. Of those that a mesh axis runs over, the one named last changes fastest.
Arguments:
- shocks: float32 [512, 512], P(('scen', 'hz'), 'trade'), may hold values from -5 to 5
- node_class: int32 [512], replicated, may hold values from 0 to 4
- positions: bfloat16 [16, 32768], P(None, ('groups', 'trade')), parts along dimension 1, may hold values from 0 to 31
- deltas: bfloat16 [16, 32768], P(None, ('groups', 'trade')), parts along dimension 1, may hold values from -0.5 to 0.5
- gammas: bfloat16 [16, 32768], P(None, ('groups', 'trade')), parts along dimension 1, may hold values from -0.5 to 0.5
- notional: bfloat16 [32768], P(('groups', 'trade')), parts along dimension 0, may hold values from -0.59765625 to 0.59765625
- block_desk: int32 [256], P(('groups', 'trade')), parts along dimension 0, may hold values from -1 to 7, as said below
Outputs:
- desk_pnl: float32 [16, 5, 512], P(('groups', 'trade'), None, ('scen', 'hz')), parts along dimension 0
The draws below stay inside these ranges and needn't reach their ends.
There are 2 independent parts, one for each index of `groups`. The reference program is written for one: setup_inputs(seed, part) draws one part's arguments, and reference() takes and returns one part's arrays. A program takes and returns all parts, laid end to end along the dimension named above; an argument that names none is the same for every part. Nothing has to cross between parts.
Inputs may be any that keep to these rules, and one draw needn't show every extreme that they name: `block_desk`: all 128 trades of a block belong to one desk; on each trade index the live blocks come first and the empty ones (-1) after them; some trade index has all 32 blocks live; summed over the trade indices, the live blocks above 24 on an index never outnumber the places left below 24 on the others.
All inputs are finite; a program needn't handle non-finite values.
Results may differ from the reference program's by a relative error of at most 0.0055.
Values may be sent and summed in bfloat16 or wider, within the bound.
A program may use at most 64 MiB of HBM per device.

```python
import jax
import jax.numpy as jnp
from jax import lax

NODES = 512
PIL = 16
BIN = 32
H = 5
BLK = 128
SLOTS = 32
HOLD = 24
DESKS = 8
SCENS = 512
TRADES = 16384
N_TRADE = 4


def draw_block_desk(key, part):
    key = jax.random.fold_in(key, 11)
    keys = jax.random.split(key, 5)
    device_order = jax.random.permutation(keys[0], N_TRADE).astype(jnp.int32)
    device_rank = jnp.argsort(device_order).astype(jnp.int32)
    is_large = device_rank < N_TRADE // 2
    large_load = jax.random.randint(keys[1], (N_TRADE,), HOLD + 1, SLOTS + 1)
    small_load = jax.random.randint(keys[2], (N_TRADE,), 1, HOLD - (SLOTS - HOLD) + 1)
    load_count = jnp.where(is_large, large_load, small_load)
    load_count = jnp.where(device_rank == 0, SLOTS, load_count)
    first_pick = jax.random.randint(keys[3], (N_TRADE, SLOTS), 0, DESKS)
    second_pick = jax.random.randint(keys[4], (N_TRADE, SLOTS), 0, DESKS)
    desk_ids = jnp.minimum(first_pick, second_pick)
    desk_ids = desk_ids.at[device_order[0], 0].set(DESKS - 1)
    live_places = jnp.arange(SLOTS, dtype=jnp.int32)[None, :] < load_count[:, None]
    return jnp.where(live_places, desk_ids, -1).reshape(-1).astype(jnp.int32)


def touch_ends(entries, own_key, least, high):
    dims = entries.shape
    place = [jax.random.randint(jax.random.fold_in(own_key, axis), (), 0, dims[axis]) for axis in range(len(dims))]
    entries = entries.at[tuple(place)].set(least)
    longest = dims.index(max(dims))
    place[longest] = (place[longest] + 1) % dims[longest]
    return entries.at[tuple(place)].set(high)


def block_scale(stream_key, dims, cuts, least, largest):
    level, own = 1.0, jax.random.fold_in(stream_key, 6)
    for axis_at, parts in cuts:
        heights = jnp.exp(jax.random.uniform(jax.random.fold_in(own, axis_at), (parts,), jnp.float32, least / len(cuts), largest / len(cuts)))
        level = level * jnp.repeat(heights, dims[axis_at] // parts).reshape([-1 if axis == axis_at else 1 for axis in range(len(dims))])
    return level


def scatter_about(stream_key, extent, deviation, limit, shards=(), kind=jnp.bfloat16):
    values = deviation * jax.random.normal(stream_key, extent, jnp.float32)
    if shards:
        values = values * block_scale(stream_key, extent, shards, -0.22, 0.18)
    return jnp.clip(values, -limit, limit).astype(kind)


def setup_inputs(seed: int = 0, part: int = 0) -> dict:
    seeds = jax.random.split(jax.random.key(seed), 8)
    part_keys = jax.random.split(jax.random.fold_in(seeds[7], part), 8)
    return {
        "shocks": scatter_about(seeds[0], (SCENS, NODES), 1.0, 5.0, ((0, 4), (1, 4)), jnp.float32),
        "node_class": touch_ends(jax.random.randint(seeds[1], (NODES,), 0, H), jax.random.fold_in(seeds[1], 1), 0, H - 1).astype(jnp.int32),
        "positions": jnp.clip(31.0 * jax.random.uniform(part_keys[2], (PIL, TRADES), jnp.float32) ** block_scale(part_keys[2], (PIL, TRADES), ((1, 4),), -0.2, 0.2), 0.0, 31.0).astype(jnp.bfloat16),
        "deltas": scatter_about(part_keys[3], (PIL, TRADES), 0.09, 0.5, ((1, 4),)),
        "gammas": scatter_about(part_keys[4], (PIL, TRADES), 0.09, 0.5, ((1, 4),)),
        "notional": scatter_about(part_keys[5], (TRADES,), 0.1, 0.59765625, ((0, 4),)),
        "block_desk": draw_block_desk(jax.random.fold_in(jax.random.fold_in(seeds[7], part), 71), part),
    }


def tables(shocks, node_class):
    horizon_mask = (node_class[None, :] >= jnp.arange(H, dtype=jnp.int32)[:, None]).astype(jnp.float32)
    linear = (horizon_mask[:, None, :] * shocks[None, :, :]).astype(jnp.bfloat16)
    square = (0.5 * horizon_mask[:, None, :] * (shocks * shocks)[None, :, :]).astype(jnp.bfloat16)
    return linear.reshape(-1, shocks.shape[1]), square.reshape(-1, shocks.shape[1])


def group_pnl(linear, square, places, delta_rows, gamma_rows, values, desk_ids, desk_total):
    node_grid = jnp.arange(BIN, dtype=jnp.float32)[None, :, None]
    weights = jnp.maximum(0.0, 1.0 - jnp.abs(node_grid - places.astype(jnp.float32)[:, None, :]))
    delta_grid = (delta_rows.astype(jnp.float32)[:, None, :] * weights).astype(jnp.bfloat16).reshape(NODES, -1)
    gamma_grid = (gamma_rows.astype(jnp.float32)[:, None, :] * weights).astype(jnp.bfloat16).reshape(NODES, -1)
    response = jnp.dot(linear, delta_grid, preferred_element_type=jnp.float32)
    response = response + jnp.dot(square, gamma_grid, preferred_element_type=jnp.float32)
    profit = values.astype(jnp.float32)[None, :] * jnp.expm1(response)
    block_sums = jnp.sum(profit.reshape(profit.shape[0], desk_ids.shape[0], -1), axis=2)
    onehot = (desk_ids[None, :] == jnp.arange(desk_total, dtype=jnp.int32)[:, None]).astype(jnp.float32)
    return jnp.einsum("db,cb->dc", onehot, block_sums, precision=lax.Precision.HIGHEST)


def reference(shocks, node_class, positions, deltas, gammas, notional, block_desk):
    linear, square = tables(shocks, node_class)
    group_blocks = SLOTS // 8
    group_rows = group_blocks * BLK
    group_count = block_desk.shape[0] // group_blocks

    def split_rows(array):
        return jnp.moveaxis(array.reshape(PIL, group_count, group_rows), 1, 0)

    stacked = (split_rows(positions), split_rows(deltas), split_rows(gammas), notional.reshape(group_count, group_rows), block_desk.reshape(group_count, group_blocks))

    def accumulate(running, pieces):
        term = group_pnl(linear, square, pieces[0], pieces[1], pieces[2], pieces[3], pieces[4], DESKS)
        return running + term, None

    running, unused = lax.scan(accumulate, jnp.zeros((DESKS, linear.shape[0]), jnp.float32), stacked)
    return running.reshape(DESKS, H, -1)
```

```python
import functools

import jax
import jax.numpy as jnp
from jax import lax
from jax.experimental import pallas as pl
from jax.experimental.pallas import tpu as pltpu
from jax.sharding import PartitionSpec as P

BIN = 32
H = 5
BLK = 128
CHUNK = 512
MESH = pl.DeviceIdType.MESH


def kernel(
    n, shocks_ref, class_ref, pos_ref, del_ref, gam_ref, val_ref, desk_ref, out_ref,
    held, table, grid, owner, total, parts, landed, send_a, recv_a, send_b, recv_b,
):
    me = lax.axis_index("trade")
    scens, cols = shocks_ref.shape
    pillars, trades = pos_ref.shape
    nodes = n * cols
    blocks = trades // BLK
    per_device = out_ref.shape[0]
    desk_rows = owner.shape[0]

    barrier = pltpu.get_barrier_semaphore()
    for off in range(1, n):
        pl.semaphore_signal(
            barrier, inc=1, device_id={"trade": lax.rem(me + off, n)}, device_id_type=MESH
        )

    own = shocks_ref[...]
    held[me, :scens, :] = own.astype(jnp.bfloat16)
    held[me, scens:, :] = (0.5 * (own * own)).astype(jnp.bfloat16)
    pl.semaphore_wait(barrier, n - 1)

    def gather_copy(slot, peer):
        return pltpu.make_async_remote_copy(
            src_ref=held.at[slot],
            dst_ref=held.at[slot],
            send_sem=send_a.at[peer],
            recv_sem=recv_a.at[slot],
            device_id={"trade": peer},
            device_id_type=MESH,
        )

    for off in range(1, n):
        gather_copy(me, lax.rem(me + off, n)).start()

    desk_iota = lax.broadcasted_iota(jnp.int32, (desk_rows, BLK), 0)

    def place_owner(b, carry):
        lanes = pl.ds(pl.multiple_of(b * BLK, BLK), BLK)
        row = val_ref[:, lanes].astype(jnp.float32)
        owner[:, lanes] = jnp.where(desk_iota == desk_ref[0, b], row, 0.0).astype(jnp.bfloat16)
        return carry

    lax.fori_loop(0, blocks, place_owner, 0)
    node_iota = lax.broadcasted_iota(jnp.int32, (BIN, CHUNK), 0).astype(jnp.float32)

    def build(c, carry):
        lanes = pl.ds(pl.multiple_of(c * CHUNK, CHUNK), CHUNK)
        pos = pos_ref[:, lanes].astype(jnp.float32)
        delta = del_ref[:, lanes].astype(jnp.float32)
        gamma = gam_ref[:, lanes].astype(jnp.float32)
        for p in range(pillars):
            weight = jnp.maximum(0.0, 1.0 - jnp.abs(node_iota - pos[p : p + 1, :]))
            grid[p * BIN : (p + 1) * BIN, lanes] = (delta[p : p + 1, :] * weight).astype(jnp.bfloat16)
            grid[nodes + p * BIN : nodes + (p + 1) * BIN, lanes] = (
                gamma[p : p + 1, :] * weight
            ).astype(jnp.bfloat16)
        return carry

    lax.fori_loop(0, trades // CHUNK, build, 0)

    for off in range(1, n):
        slot = lax.rem(me + n - off, n)
        gather_copy(slot, slot).wait_recv()
    for h in range(H):
        live = (class_ref[...] >= h).astype(jnp.float32).astype(jnp.bfloat16)
        line = jnp.concatenate([held[k, :scens, :] for k in range(n)], axis=1)
        table[h * scens : (h + 1) * scens, :nodes] = line * live
        line = jnp.concatenate([held[k, scens:, :] for k in range(n)], axis=1)
        table[h * scens : (h + 1) * scens, nodes:] = line * live

    total[...] = jnp.zeros_like(total)

    def value(c, carry):
        lanes = pl.ds(pl.multiple_of(c * CHUNK, CHUNK), CHUNK)
        response = jnp.dot(table[...], grid[:, lanes], preferred_element_type=jnp.float32)
        growth = (jnp.exp(response) - 1.0).astype(jnp.bfloat16)
        total[...] += lax.dot_general(
            owner[:, lanes], growth, (((1,), (1,)), ((), ())), preferred_element_type=jnp.float32
        )
        return carry

    lax.fori_loop(0, trades // CHUNK, value, 0)

    for k in range(n):
        for d in range(per_device):
            for h in range(H):
                parts[k, d, h : h + 1, :] = total[
                    k * per_device + d : k * per_device + d + 1, h * scens : (h + 1) * scens
                ]

    def share_copy(slot, peer):
        return pltpu.make_async_remote_copy(
            src_ref=parts.at[peer],
            dst_ref=landed.at[slot],
            send_sem=send_b.at[peer],
            recv_sem=recv_b.at[slot],
            device_id={"trade": peer},
            device_id_type=MESH,
        )

    for off in range(1, n):
        share_copy(me, lax.rem(me + off, n)).start()
    result = parts[me]
    for off in range(1, n):
        slot = lax.rem(me + n - off, n)
        share_copy(slot, slot).wait_recv()
        result = result + landed[slot]
    out_ref[...] = result[:, :H, :]
    for off in range(1, n):
        peer = lax.rem(me + off, n)
        gather_copy(me, peer).wait_send()
        share_copy(me, peer).wait_send()


def body(shocks, node_class, positions, deltas, gammas, notional, block_desk):
    n = lax.axis_size("trade")
    scens, cols = shocks.shape
    pillars, trades = positions.shape
    nodes = n * cols
    per_device = 2
    desk_rows = -(-(per_device * n) // 16) * 16
    vmem = pl.BlockSpec(memory_space=pltpu.VMEM)
    return pl.pallas_call(
        functools.partial(kernel, n),
        out_shape=jax.ShapeDtypeStruct((per_device, H, scens), jnp.float32),
        in_specs=[vmem] * 6 + [pl.BlockSpec(memory_space=pltpu.SMEM)],
        out_specs=vmem,
        scratch_shapes=[
            pltpu.VMEM((n, 2 * scens, cols), jnp.bfloat16),
            pltpu.VMEM((H * scens, 2 * nodes), jnp.bfloat16),
            pltpu.VMEM((2 * nodes, trades), jnp.bfloat16),
            pltpu.VMEM((desk_rows, trades), jnp.bfloat16),
            pltpu.VMEM((desk_rows, H * scens), jnp.float32),
            pltpu.VMEM((n, per_device, 8, scens), jnp.float32),
            pltpu.VMEM((n, per_device, 8, scens), jnp.float32),
            pltpu.SemaphoreType.DMA((n,)),
            pltpu.SemaphoreType.DMA((n,)),
            pltpu.SemaphoreType.DMA((n,)),
            pltpu.SemaphoreType.DMA((n,)),
        ],
        compiler_params=pltpu.CompilerParams(
            collective_id=0, has_side_effects=True, vmem_limit_bytes=40 * 1024 * 1024
        ),
    )(
        shocks,
        node_class.reshape(1, -1),
        positions,
        deltas,
        gammas,
        notional.reshape(1, -1),
        block_desk.reshape(1, -1),
    )


def solution(mesh):
    in_specs = (
        P(("scen", "hz"), "trade"),
        P(),
        P(None, ("groups", "trade")),
        P(None, ("groups", "trade")),
        P(None, ("groups", "trade")),
        P(("groups", "trade")),
        P(("groups", "trade")),
    )
    out_specs = P(("groups", "trade"), None, ("scen", "hz"))
    return jax.shard_map(body, mesh=mesh, in_specs=in_specs, out_specs=out_specs, check_vma=False)
```

```python
import functools

import jax
import jax.numpy as jnp
from jax import lax
from jax.experimental import pallas as pl
from jax.experimental.pallas import tpu as pltpu
from jax.sharding import PartitionSpec as P

BIN = 32
H = 5
BLK = 128
CHUNK = 1024
SUB = 256
VLIM = 60
MESH = pl.DeviceIdType.MESH


def kernel(
    n, shocks_hbm, class_ref, pos_hbm, del_hbm, gam_hbm, val_hbm, desk_ref, out_ref,
    shocks_ref, pos_ref, del_ref, gam_ref, val_ref, load_sem, held, table, grid, owner, total, even, odd, parts, landed, send_a, recv_a, send_b, recv_b, swap_sem,
):
    me = lax.axis_index("trade")
    side = lax.axis_index("groups")
    scens, cols = shocks_ref.shape
    pillars, trades = pos_ref.shape
    nodes = n * cols
    rows = scens // 2
    blocks = trades // BLK
    per_device = out_ref.shape[0]
    desk_rows = owner.shape[0]

    loads = [
        pltpu.make_async_copy(source, target, load_sem.at[i])
        for i, (source, target) in enumerate(
            [
                (shocks_hbm, shocks_ref),
                (val_hbm, val_ref),
                (pos_hbm, pos_ref),
                (del_hbm, del_ref),
                (gam_hbm, gam_ref),
            ]
        )
    ]
    for load in loads:
        load.start()
    barrier = pltpu.get_barrier_semaphore()
    for off in range(1, n):
        pl.semaphore_signal(
            barrier, inc=1, device_id={"trade": lax.rem(me + off, n)}, device_id_type=MESH
        )

    pl.semaphore_signal(
        barrier, inc=1, device_id={"groups": 1 - side}, device_id_type=MESH
    )
    loads[0].wait()
    own = shocks_ref[pl.ds(pl.multiple_of(side * rows, rows), rows), :]
    held[side, me, :rows, :] = own.astype(jnp.bfloat16)
    held[side, me, rows:, :] = (0.5 * (own * own)).astype(jnp.bfloat16)
    pl.semaphore_wait(barrier, n)

    def gather_copy(slot, peer):
        return pltpu.make_async_remote_copy(
            src_ref=held.at[side, slot],
            dst_ref=held.at[side, slot],
            send_sem=send_a.at[peer],
            recv_sem=recv_a.at[slot],
            device_id={"trade": peer},
            device_id_type=MESH,
        )

    def swap_copy(half):
        return pltpu.make_async_remote_copy(
            src_ref=held.at[half],
            dst_ref=held.at[half],
            send_sem=swap_sem.at[0],
            recv_sem=swap_sem.at[1],
            device_id={"groups": 1 - side},
            device_id_type=MESH,
        )

    for off in range(1, n):
        gather_copy(me, lax.rem(me + off, n)).start()

    for load in loads[1:]:
        load.wait()

    desk_iota = lax.broadcasted_iota(jnp.int32, (desk_rows, BLK), 0)

    values = val_ref[...].astype(jnp.float32).reshape(1, trades)
    for b in range(blocks):
        row = values[:, b * BLK : (b + 1) * BLK]
        owner[:, b * BLK : (b + 1) * BLK] = jnp.where(desk_iota == desk_ref[b], row, 0.0).astype(
            jnp.bfloat16
        )
    node_iota = lax.broadcasted_iota(jnp.int32, (BIN, CHUNK), 0).astype(jnp.float32)

    def build(c, carry):
        lanes = pl.ds(pl.multiple_of(c * CHUNK, CHUNK), CHUNK)
        pos = pos_ref[:, lanes].astype(jnp.float32)
        delta = del_ref[:, lanes].astype(jnp.float32)
        gamma = gam_ref[:, lanes].astype(jnp.float32)
        for p in range(pillars):
            weight = jnp.maximum(0.0, 1.0 - jnp.abs(node_iota - pos[p : p + 1, :]))
            grid[p * BIN : (p + 1) * BIN, lanes] = (delta[p : p + 1, :] * weight).astype(jnp.bfloat16)
            grid[nodes + p * BIN : nodes + (p + 1) * BIN, lanes] = (
                gamma[p : p + 1, :] * weight
            ).astype(jnp.bfloat16)
        return carry

    lax.fori_loop(0, trades // CHUNK, build, 0)

    def receive(turn):
        half = lax.rem(side + turn, 2)
        if turn == 0:
            for off in range(1, n):
                slot = lax.rem(me + n - off, n)
                gather_copy(slot, slot).wait_recv()
            swap_copy(half).start()
        else:
            swap_copy(half).wait_recv()
        line = jnp.concatenate([held[half, k, :rows, :] for k in range(n)], axis=1)
        curve = jnp.concatenate([held[half, k, rows:, :] for k in range(n)], axis=1)
        for h in range(H):
            live = (class_ref[...] >= h).astype(jnp.float32).astype(jnp.bfloat16)
            table[turn, h * rows : (h + 1) * rows, :nodes] = line * live
            table[turn, h * rows : (h + 1) * rows, nodes:] = curve * live

    total[...] = jnp.zeros_like(total)

    def respond(half, c, into, part):
        lanes = pl.ds(pl.multiple_of(c * CHUNK + part * SUB, SUB), SUB)
        into[:, part * SUB : (part + 1) * SUB] = jnp.dot(
            table[half], grid[:, lanes], preferred_element_type=jnp.float32
        )

    def settle(half, c, held_response, part):
        lanes = pl.ds(pl.multiple_of(c * CHUNK + part * SUB, SUB), SUB)
        growth = jnp.exp(held_response[:, part * SUB : (part + 1) * SUB]) - 1.0
        total[half] += lax.dot_general(
            owner[:, lanes],
            growth.astype(jnp.bfloat16),
            (((1,), (1,)), ((), ())),
            preferred_element_type=jnp.float32,
        )

    parts_of_chunk = CHUNK // SUB
    chunks = trades // CHUNK

    def advance(half, c, old, new):
        for part in range(parts_of_chunk):
            respond(half, c + 1, new, part)
            settle(half, c, old, part)

    def sweep(half):
        def pair(i, carry):
            advance(half, 2 * i, even, odd)
            advance(half, 2 * i + 1, odd, even)
            return carry

        lax.fori_loop(0, chunks // 2 - 1, pair, 0)
        advance(half, chunks - 2, even, odd)

    receive(0)
    for part in range(parts_of_chunk):
        respond(0, 0, even, part)
    sweep(0)
    receive(1)
    for part in range(parts_of_chunk):
        respond(1, 0, even, part)
        settle(0, chunks - 1, odd, part)
    sweep(1)
    for part in range(parts_of_chunk):
        settle(1, chunks - 1, odd, part)

    for k in range(n):
        for d in range(per_device):
            for h in range(H):
                row = k * per_device + d
                parts[k, d, h : h + 1, :] = jnp.concatenate(
                    [total[lax.rem(side + half, 2), row : row + 1, h * rows : (h + 1) * rows] for half in range(2)],
                    axis=1,
                )

    def share_copy(slot, peer):
        return pltpu.make_async_remote_copy(
            src_ref=parts.at[peer],
            dst_ref=landed.at[slot],
            send_sem=send_b.at[peer],
            recv_sem=recv_b.at[slot],
            device_id={"trade": peer},
            device_id_type=MESH,
        )

    for off in range(1, n):
        share_copy(me, lax.rem(me + off, n)).start()
    result = parts[me]
    for off in range(1, n):
        slot = lax.rem(me + n - off, n)
        share_copy(slot, slot).wait_recv()
        result = result + landed[slot]
    out_ref[...] = result[:, :H, :]
    for off in range(1, n):
        peer = lax.rem(me + off, n)
        gather_copy(me, peer).wait_send()
        share_copy(me, peer).wait_send()
    swap_copy(side).wait_send()


def body(shocks, node_class, positions, deltas, gammas, notional, block_desk):
    n = lax.axis_size("trade")
    scens, cols = shocks.shape
    pillars, trades = positions.shape
    nodes = n * cols
    per_device = 2
    desk_rows = -(-(per_device * n) // 16) * 16
    hbm = pl.BlockSpec(memory_space=pltpu.HBM)
    vmem = pl.BlockSpec(memory_space=pltpu.VMEM)
    return pl.pallas_call(
        functools.partial(kernel, n),
        out_shape=jax.ShapeDtypeStruct((per_device, H, scens), jnp.float32),
        in_specs=[hbm, vmem, hbm, hbm, hbm, hbm, pl.BlockSpec(memory_space=pltpu.SMEM)],
        out_specs=vmem,
        scratch_shapes=[
            pltpu.VMEM((scens, cols), jnp.float32),
            pltpu.VMEM((pillars, trades), jnp.bfloat16),
            pltpu.VMEM((pillars, trades), jnp.bfloat16),
            pltpu.VMEM((pillars, trades), jnp.bfloat16),
            pltpu.VMEM((trades,), jnp.bfloat16),
            pltpu.SemaphoreType.DMA((5,)),
            pltpu.VMEM((2, n, scens, cols), jnp.bfloat16),
            pltpu.VMEM((2, H * scens // 2, 2 * nodes), jnp.bfloat16),
            pltpu.VMEM((2 * nodes, trades), jnp.bfloat16),
            pltpu.VMEM((desk_rows, trades), jnp.bfloat16),
            pltpu.VMEM((2, desk_rows, H * scens // 2), jnp.float32),
            pltpu.VMEM((H * scens // 2, CHUNK), jnp.float32),
            pltpu.VMEM((H * scens // 2, CHUNK), jnp.float32),
            pltpu.VMEM((n, per_device, 8, scens), jnp.float32),
            pltpu.VMEM((n, per_device, 8, scens), jnp.float32),
            pltpu.SemaphoreType.DMA((n,)),
            pltpu.SemaphoreType.DMA((n,)),
            pltpu.SemaphoreType.DMA((n,)),
            pltpu.SemaphoreType.DMA((n,)),
            pltpu.SemaphoreType.DMA((2,)),
        ],
        compiler_params=pltpu.CompilerParams(
            collective_id=0, has_side_effects=True, vmem_limit_bytes=VLIM * 1024 * 1024
        ),
    )(
        shocks,
        node_class.reshape(1, -1),
        positions,
        deltas,
        gammas,
        notional,
        block_desk,
    )


def solution(mesh):
    in_specs = (
        P(("scen", "hz"), "trade"),
        P(),
        P(None, ("groups", "trade")),
        P(None, ("groups", "trade")),
        P(None, ("groups", "trade")),
        P(("groups", "trade")),
        P(("groups", "trade")),
    )
    out_specs = P(("groups", "trade"), None, ("scen", "hz"))
    return jax.shard_map(body, mesh=mesh, in_specs=in_specs, out_specs=out_specs, check_vma=False)
```
